32 devices in a mesh: seq: 8 (over z, y), tp: 4 (over x, core).
Axes of the slice: x: 2, y: 2, z: 4, core: 2. Of those that a mesh axis runs over, the one named last changes fastest.
Arguments:
- hidden: bfloat16 [8192, 2048], P('seq', 'tp'), may hold values from -6 to 6
- x_weight: bfloat16 [2048, 4096], P(None, 'tp'), may hold values from -0.125 to 0.125
- z_weight: bfloat16 [2048, 4096], P(None, 'tp'), may hold values from -0.125 to 0.125
- bc_weight: bfloat16 [2048, 256], P(None, 'tp'), may hold values from -0.125 to 0.125
- dt_weight: bfloat16 [2048, 64], P(None, 'tp'), may hold values from -0.125 to 0.125
- conv_x: float32 [4, 4096], P(None, 'tp'), may hold values from -3 to 3
- conv_bc: float32 [4, 256], replicated, may hold values from -3 to 3
- dt_bias: float32 [64], P('tp'), may hold values from -2 to 1
- decay_rate: float32 [64], P('tp'), may hold values from 2e-05 to 0.2
- skip_gain: float32 [64], P('tp'), may hold values from 0.2 to 1.5
- norm_gain: float32 [4096], P('tp'), may hold values from 0.5 to 1.5
- out_weight: bfloat16 [4096, 2048], P('tp'), may hold values from -0.09375 to 0.09375
- lengths: int32 [4], replicated, may hold values from 1 to 4096, as said below
- owners: int32 [8], P('seq'), may hold values from 0 to 3, as said below
Outputs:
- mixed: bfloat16 [8192, 2048], P('seq', 'tp')
- final_state: float32 [8, 64, 64, 128], P('seq', 'tp')
- conv_edge_x: bfloat16 [8, 3, 4096], P('seq', None, 'tp')
- conv_edge_bc: bfloat16 [8, 3, 256], P('seq')
The draws below stay inside these ranges and needn't reach their ends.
Inputs may be any that keep to these rules, and one draw needn't show every extreme that they name: The prompts are packed in order and their lengths sum to 8192; the second prompt is the longest and holds exactly half of 8192 tokens; the third and fourth together hold at least 3 tokens, and one of them holds one or two. `owners`: every prompt is kept by the same number of indices.
All inputs are finite; a program needn't handle non-finite values.
Results may differ from the reference program's by a relative error of at most 0.013.
Values may be sent and summed in bfloat16 or wider, within the bound.
A program may use at most 192 MiB of HBM per device.

```python
import math
import jax
import jax.numpy as jnp
from jax import lax

D = 2048
HEADS = 64
HDIM = 64
NS = 128
KCONV = 4
GROUP = 256
PROMPTS = 4
DIN = 4096
TOKENS = 8192
N_SEQ = 8


def draw_owners(key, part):
    order = jax.random.permutation(key, N_SEQ)
    return (order % PROMPTS).astype(jnp.int32)


def draw_lengths(key, part):
    half = TOKENS // 2
    key_first, key_short, key_slot = jax.random.split(key, 3)
    first_len = jax.random.randint(key_first, (), 1, half - KCONV + 2).astype(jnp.int32)
    short_len = jax.random.randint(key_short, (), 1, 3).astype(jnp.int32)
    other_len = (half - first_len - short_len).astype(jnp.int32)
    slot = jax.random.randint(key_slot, (), 0, 2).astype(jnp.int32)
    third = jnp.where(slot == 0, short_len, other_len)
    fourth = jnp.where(slot == 0, other_len, short_len)
    head = jnp.stack([first_len, jnp.asarray(half, jnp.int32), third, fourth]).astype(jnp.int32)
    filler = jnp.ones((PROMPTS - 4,), jnp.int32) if PROMPTS > 4 else jnp.zeros((0,), jnp.int32)
    return jnp.concatenate([head, filler])[:PROMPTS].astype(jnp.int32)


def levels(stream_key, dims, shards, smallest, top_value):
    def one(dim, parts):
        draws = jax.random.uniform(jax.random.fold_in(jax.random.fold_in(stream_key, 6), dim), (parts,), jnp.float32, smallest / len(shards), top_value / len(shards))
        return jnp.repeat(jnp.exp(draws), dims[dim] // parts).reshape((-1,) + (1,) * (len(dims) - dim - 1))

    loudness = one(*shards[0])
    for cut in shards[1:]:
        loudness = loudness * one(*cut)
    return loudness


def normal_values(own_key, shape, scale, most, cuts=(), held_as=jnp.bfloat16):
    array = scale * jax.random.normal(own_key, shape, jnp.float32)
    if cuts:
        array = array * levels(own_key, shape, cuts, -0.22, 0.18)
    return jnp.clip(array, -most, most).astype(held_as)


def setup_inputs(seed: int = 0) -> dict:
    key_of = jax.random.split(jax.random.key(seed), 15)
    hidden = normal_values(key_of[0], (TOKENS, D), 1.0, 6.0, ((0, 8), (1, 4)))
    x_weight = normal_values(key_of[1], (D, DIN), D ** -0.5, 0.125, ((1, 4),))
    z_weight = normal_values(key_of[2], (D, DIN), D ** -0.5, 0.125, ((1, 4),))
    bc_weight = normal_values(key_of[3], (D, 2 * NS), D ** -0.5, 0.125, ((1, 4),))
    dt_weight = normal_values(key_of[4], (D, HEADS), D ** -0.5, 0.125, ((1, 4),))
    conv_x = normal_values(key_of[5], (KCONV, DIN), KCONV ** -0.5, 3.0, ((1, 4),), jnp.float32)
    conv_bc = normal_values(key_of[6], (KCONV, 2 * NS), KCONV ** -0.5, 3.0, (), jnp.float32)
    dt_bias = jnp.clip(-2.0 + 3.0 * jax.random.uniform(key_of[7], (HEADS,), jnp.float32) ** levels(key_of[7], (HEADS,), ((0, 4),), -0.2, 0.2), -2.0, 1.0)
    decay_rate = jnp.clip(jnp.exp(math.log(0.2) - 9.2103404 * jax.random.uniform(key_of[8], (HEADS,), jnp.float32) ** levels(key_of[8], (HEADS,), ((0, 4),), -0.2, 0.2)), 1.9999999494757503e-05, 0.2)
    skip_gain = jnp.clip(0.2 + 1.3 * jax.random.uniform(key_of[9], (HEADS,), jnp.float32) ** levels(key_of[9], (HEADS,), ((0, 4),), -0.2, 0.2), 0.2, 1.5)
    norm_gain = jnp.clip(1.0 + 0.1 * jax.random.normal(key_of[10], (DIN,), jnp.float32), 0.5, 1.5)
    out_weight = normal_values(key_of[11], (DIN, D), DIN ** -0.5, 0.09375, ((0, 4),))
    lengths = draw_lengths(jax.random.fold_in(key_of[14], 71), 0)
    owners = draw_owners(jax.random.fold_in(key_of[14], 71), 0)
    return dict(hidden=hidden, x_weight=x_weight, z_weight=z_weight, bc_weight=bc_weight, dt_weight=dt_weight, conv_x=conv_x, conv_bc=conv_bc, dt_bias=dt_bias, decay_rate=decay_rate, skip_gain=skip_gain, norm_gain=norm_gain, out_weight=out_weight, lengths=lengths, owners=owners)


highest = lax.Precision.HIGHEST
epsilon = 1e-05

def segment_of(positions, prompt_end):
    counted = lax.optimization_barrier(jnp.sum((positions[:, None] >= prompt_end[None, :]).astype(jnp.int32), axis=1))
    return jnp.where(positions < 0, -1, counted).astype(jnp.int32)

def short_conv(extended, seg_ext, kernel):
    taps = kernel.shape[0]
    count = extended.shape[0] - taps + 1
    total = jnp.zeros((count, extended.shape[1]), jnp.float32)
    for offset in range(taps):
        same = (seg_ext[offset:offset + count] == seg_ext[taps - 1:]).astype(jnp.float32)
        total = total + extended[offset:offset + count].astype(jnp.float32) * kernel[offset][None, :] * same[:, None]
    return jax.nn.silu(total).astype(jnp.bfloat16)

def advance_block(state, block):
    x_blk, b_blk, c_blk, dt_blk, log_blk, seg_blk, seg_prior = block
    length = seg_blk.shape[0]
    acum = jnp.cumsum(log_blk, axis=0)
    index = jnp.arange(length, dtype=jnp.int32)
    keep = (seg_blk[:, None] == seg_blk[None, :]) & (index[:, None] >= index[None, :])
    spread = acum[:, None, :] - acum[None, :, :]
    decay = jnp.where(keep[:, :, None], jnp.exp(jnp.where(keep[:, :, None], spread, 0.0)), 0.0)
    scores = jnp.dot(c_blk, b_blk.T, precision=highest)
    mixing = scores[:, :, None] * decay * dt_blk[None, :, :]
    output = jnp.einsum('ijh,jhp->ihp', mixing, x_blk, precision=highest)
    inflow = jnp.where((seg_blk == seg_prior)[:, None], jnp.exp(acum), 0.0)
    output = output + inflow[:, :, None] * jnp.einsum('in,hpn->ihp', c_blk, state, precision=highest)
    closing = seg_blk[length - 1]
    tail = jnp.where((seg_blk == closing)[:, None], jnp.exp(acum[length - 1][None, :] - acum), 0.0) * dt_blk
    fresh = jnp.einsum('jh,jhp,jn->hpn', tail, x_blk, b_blk, precision=highest)
    carry = jnp.where(closing == seg_prior, jnp.exp(acum[length - 1]), 0.0)
    return (carry[:, None, None] * state + fresh, (output, state))

def state_at(start_state, seg_prior, x_rows, b_rows, dt_rows, log_rows, seg_rows, inner, prompt):
    acum = jnp.cumsum(log_rows, axis=0)
    level = acum[inner]
    index = jnp.arange(seg_rows.shape[0], dtype=jnp.int32)
    chosen = (seg_rows == prompt) & (index <= inner)
    weight = jnp.where(chosen[:, None], jnp.exp(jnp.where(chosen[:, None], level[None, :] - acum, 0.0)), 0.0) * dt_rows
    inflow = jnp.where(seg_rows[inner] == seg_prior, jnp.exp(level), 0.0)
    return inflow[:, None, None] * start_state + jnp.einsum('jh,jhp,jn->hpn', weight, x_rows, b_rows, precision=highest)

def reference(hidden, x_weight, z_weight, bc_weight, dt_weight, conv_x, conv_bc, dt_bias, decay_rate, skip_gain, norm_gain, out_weight, lengths, owners):
    total_rows = hidden.shape[0]
    prompt_end = jnp.cumsum(lengths).astype(jnp.int32)
    prompt_start = (prompt_end - lengths).astype(jnp.int32)
    positions = jnp.arange(total_rows, dtype=jnp.int32)
    segment = segment_of(positions, prompt_end)
    x_in = jnp.dot(hidden, x_weight, preferred_element_type=jnp.float32).astype(jnp.bfloat16)
    z_in = jnp.dot(hidden, z_weight, preferred_element_type=jnp.float32).astype(jnp.bfloat16)
    bc_in = jnp.dot(hidden, bc_weight, preferred_element_type=jnp.float32).astype(jnp.bfloat16)
    dt_raw = jnp.dot(hidden, dt_weight, preferred_element_type=jnp.float32)
    joined = jnp.concatenate([x_in, bc_in], axis=1)
    extended = jnp.concatenate([jnp.zeros((KCONV - 1, joined.shape[1]), jnp.bfloat16), joined], axis=0)
    seg_ext = jnp.concatenate([jnp.full((KCONV - 1,), -1, jnp.int32), segment])
    kernel = jnp.concatenate([conv_x, conv_bc], axis=1)
    mixed_in = short_conv(extended, seg_ext, kernel)
    x_conv = mixed_in[:, :DIN].astype(jnp.float32).reshape(total_rows, HEADS, HDIM)
    b_conv = mixed_in[:, DIN:DIN + NS].astype(jnp.float32)
    c_conv = mixed_in[:, DIN + NS:].astype(jnp.float32)
    step_size = jax.nn.softplus(dt_raw + dt_bias[None, :])
    log_decay = -decay_rate[None, :] * step_size
    blocks = total_rows // GROUP
    block_first = jnp.arange(blocks, dtype=jnp.int32) * GROUP
    seg_prior = segment_of(block_first - 1, prompt_end)
    x_blocks = x_conv.reshape(blocks, GROUP, HEADS, HDIM)
    b_blocks = b_conv.reshape(blocks, GROUP, NS)
    c_blocks = c_conv.reshape(blocks, GROUP, NS)
    dt_blocks = step_size.reshape(blocks, GROUP, HEADS)
    log_blocks = log_decay.reshape(blocks, GROUP, HEADS)
    seg_blocks = segment.reshape(blocks, GROUP)
    init_state = jnp.zeros((HEADS, HDIM, NS), jnp.float32)
    packed = (x_blocks, b_blocks, c_blocks, dt_blocks, log_blocks, seg_blocks, seg_prior)
    unused, (outputs, priors) = lax.scan(advance_block, init_state, packed)
    ssm = outputs.reshape(total_rows, HEADS, HDIM) + skip_gain[None, :, None] * x_conv
    gated = ssm.reshape(total_rows, DIN) * jax.nn.silu(z_in.astype(jnp.float32))
    mean_sq = lax.optimization_barrier(jnp.sum(gated * gated, axis=1)) / DIN
    normed = (gated * lax.rsqrt(mean_sq + epsilon)[:, None] * norm_gain[None, :]).astype(jnp.bfloat16)
    mixed = jnp.dot(normed, out_weight, preferred_element_type=jnp.float32).astype(jnp.bfloat16)
    last_row = prompt_end - 1
    finals = []
    edges = []
    for prompt in range(PROMPTS):
        row = last_row[prompt]
        block_id = row // GROUP
        inner = (row - block_id * GROUP).astype(jnp.int32)
        finals.append(state_at(priors[block_id], seg_prior[block_id], x_blocks[block_id], b_blocks[block_id], dt_blocks[block_id], log_blocks[block_id], seg_blocks[block_id], inner, prompt))
        window = lax.dynamic_slice_in_dim(extended, (row + 1).astype(jnp.int32), KCONV - 1, 0)
        rows_global = row - (KCONV - 2) + jnp.arange(KCONV - 1, dtype=jnp.int32)
        valid = rows_global >= prompt_start[prompt]
        edges.append(jnp.where(valid[:, None], window, jnp.zeros_like(window)))
    final_all = jnp.stack(finals)
    edge_all = jnp.stack(edges)
    final_state = final_all[owners]
    edge_kept = edge_all[owners]
    return (mixed, final_state, edge_kept[:, :, :DIN], edge_kept[:, :, DIN:])
```

```python
import functools

import jax
import jax.numpy as jnp
from jax import lax
from jax.experimental import pallas as pl
from jax.experimental.pallas import tpu as pltpu
from jax.sharding import PartitionSpec as P

NS = 128
KCONV = 4
PROMPTS = 4
DIN = 4096
CHUNK = 128
LANES = 128
HALO = 16
EXTRA = 16
NEVER = -1e30

epsilon = 1e-05
f32 = jnp.float32
bf16 = jnp.bfloat16


def rows_iota(rows, columns=LANES):
    return lax.broadcasted_iota(jnp.int32, (rows, columns), 0)


def start_of(position, place_ref):
    start = jnp.zeros_like(position)
    for r in range(PROMPTS):
        start = jnp.where(position >= place_ref[r], place_ref[r], start)
    return start


def split(value):
    high = value.astype(bf16)
    return high, (value - high.astype(f32)).astype(bf16)


def spread_heads(value, expand_ref):
    high, low = split(value)
    return jnp.dot(
        jnp.concatenate([high, low], axis=1), expand_ref[...], preferred_element_type=f32
    )


def spread_row(row, expand_ref):
    return spread_heads(jnp.broadcast_to(row, (16, LANES)), expand_ref)[0:1]


def split_rows(row, first, expand_ref):
    high, low = split(jnp.broadcast_to(row, (EXTRA, LANES)))
    at = rows_iota(EXTRA)
    both = jnp.where(at == first, high.astype(f32), 0.0) + jnp.where(
        at == first + 1, low.astype(f32), 0.0
    )
    return jnp.dot(both.astype(bf16), expand_ref[0:LANES], preferred_element_type=f32)


def conv_columns(ext_ref, taps_ref, columns, age):
    total = ext_ref[HALO : HALO + CHUNK, columns] * taps_ref[KCONV - 1 : KCONV, columns]
    for back in range(1, KCONV):
        term = (
            ext_ref[HALO - back : HALO - back + CHUNK, columns]
            * taps_ref[KCONV - 1 - back : KCONV - back, columns]
        )
        total = total + jnp.where(age >= back, term, 0.0)
    return (total * jax.nn.sigmoid(total)).astype(bf16)


def states_kernel(
    place_ref, x_ref, bc_ref, halo_x_ref, halo_bc_ref, dt_ref, taps_x_ref, taps_bc_ref,
    bias_ref, rate_ref, expand_ref,
    xc_ref, xdt_ref, bcc_ref, acum_ref, prior_ref, thr_ref, end_ref, finals_ref,
    ext_x, ext_bc, state, through,
):
    step = pl.program_id(0)
    width = x_ref.shape[1]

    @pl.when(step == 0)
    def _():
        ext_x[0:HALO] = halo_x_ref[...].astype(f32)
        ext_bc[0:HALO] = halo_bc_ref[...].astype(f32)
        state[...] = jnp.zeros_like(state)
        through[...] = jnp.ones_like(through)
        finals_ref[...] = jnp.zeros_like(finals_ref)

    @pl.when(step > 0)
    def _():
        ext_x[0:HALO] = ext_x[CHUNK : CHUNK + HALO]
        ext_bc[0:HALO] = ext_bc[CHUNK : CHUNK + HALO]

    ext_x[HALO : HALO + CHUNK] = x_ref[...].astype(f32)
    ext_bc[HALO : HALO + CHUNK] = bc_ref[...].astype(f32)

    first = place_ref[2 * PROMPTS] + step * CHUNK
    local = rows_iota(CHUNK)
    token = first + local
    age = token - start_of(token, place_ref)
    for tile in range(width // LANES):
        columns = slice(tile * LANES, (tile + 1) * LANES)
        xc_ref[:, columns] = conv_columns(ext_x, taps_x_ref, columns, age)
    for tile in range(2 * NS // LANES):
        columns = slice(tile * LANES, (tile + 1) * LANES)
        bcc_ref[:, columns] = conv_columns(ext_bc, taps_bc_ref, columns, age)

    raw = dt_ref[...] + bias_ref[0:1]
    dt = jnp.maximum(raw, 0.0) + jnp.log1p(jnp.exp(-jnp.abs(raw)))
    log_decay = -rate_ref[0:1] * dt
    lower = (
        local >= lax.broadcasted_iota(jnp.int32, (CHUNK, CHUNK), 1)
    ).astype(f32)
    acum = jnp.dot(
        lower, log_decay, precision=lax.Precision.HIGHEST, preferred_element_type=f32
    )
    acum_ref[...] = acum
    x_dt = xc_ref[...].astype(f32) * spread_heads(dt, expand_ref)
    xdt_ref[...] = x_dt.astype(bf16)
    b_turned = jnp.transpose(bcc_ref[:, 0:NS].astype(f32)).astype(bf16)
    prior_ref[0] = state[...].astype(bf16)
    thr_ref[0] = through[...]

    for r in range(PROMPTS):
        inner = place_ref[r] - 1 - first
        begin = place_ref[PROMPTS + r]

        @pl.when((inner >= 0) & (inner < CHUNK))
        def _():
            level = jnp.sum(jnp.where(local == inner, acum, 0.0), axis=0, keepdims=True)
            chosen = (local <= inner) & (token >= begin)
            weight = jnp.exp(jnp.where(chosen, level - acum, NEVER))
            enter = jnp.exp(level) * (begin < first).astype(f32)
            rows = (x_dt * spread_heads(weight, expand_ref)).astype(bf16)
            finals_ref[r, 0:NS] = (
                spread_row(enter, expand_ref) * state[...]
                + jnp.dot(b_turned, rows, preferred_element_type=f32)
            ).astype(bf16)
            at = rows_iota(EXTRA, HALO + CHUNK)
            place = lax.broadcasted_iota(jnp.int32, (EXTRA, HALO + CHUNK), 1)
            count = KCONV - 1

            def pick(skip):
                wanted = inner - (count - 1) + at - skip
                ok = (at >= skip) & (at < skip + count) & (first + wanted >= begin)
                return jnp.where(ok & (place == HALO + wanted), 1.0, 0.0).astype(bf16)

            edge_x = jnp.dot(pick(0), ext_x[...].astype(bf16), preferred_element_type=f32)
            edge_bc = jnp.dot(pick(count), ext_bc[...].astype(bf16), preferred_element_type=f32)
            edge_bc = jnp.concatenate(
                [edge_bc, jnp.zeros((EXTRA, width - 2 * NS), f32)], axis=1
            )
            passing = split_rows(through[0:1] * enter, 2 * count, expand_ref)
            finals_ref[r, NS : NS + EXTRA] = (edge_x + edge_bc + passing).astype(bf16)

    last = acum[CHUNK - 1 : CHUNK]
    closing = start_of(first + CHUNK - 1, place_ref)
    tail = jnp.exp(jnp.where(token >= closing, last - acum, NEVER))
    carry = jnp.exp(last) * (closing < first).astype(f32)
    rows = (x_dt * spread_heads(tail, expand_ref)).astype(bf16)
    state[...] = spread_row(carry, expand_ref) * state[...] + jnp.dot(
        b_turned, rows, preferred_element_type=f32
    )
    through[...] = through[...] * carry

    @pl.when(step == pl.num_programs(0) - 1)
    def _():
        end_ref[0:NS] = state[...].astype(bf16)
        end_ref[NS : NS + EXTRA] = split_rows(through[0:1], 0, expand_ref).astype(bf16)


def within_kernel(place_ref, xc_ref, xdt_ref, bcc_ref, acum_ref, skip_ref, y_ref):
    width = xc_ref.shape[1]
    first = place_ref[2 * PROMPTS] + pl.program_id(0) * CHUNK
    local = rows_iota(CHUNK)
    token = first + local
    age = token - start_of(token, place_ref)
    behind = local - lax.broadcasted_iota(jnp.int32, (CHUNK, CHUNK), 1)
    bias = jnp.where((behind >= 0) & (behind <= age), 0.0, NEVER)
    scores = lax.dot_general(
        bcc_ref[:, NS:], bcc_ref[:, :NS], (((1,), (1,)), ((), ())), preferred_element_type=f32
    )
    acum = acum_ref[...]
    acum_turned = jnp.transpose(acum)
    low_half = lax.broadcasted_iota(jnp.int32, (CHUNK, LANES), 1) < LANES // 2
    for pair in range(width // LANES):
        columns = slice(pair * LANES, (pair + 1) * LANES)
        mixing = []
        for head in (2 * pair, 2 * pair + 1):
            spread = acum[:, head : head + 1] - acum_turned[head : head + 1] + bias
            mixing.append((jnp.exp(spread) * scores).astype(bf16))
        x_dt = xdt_ref[:, columns].astype(f32)
        stacked = jnp.concatenate(
            [jnp.where(low_half, x_dt, 0.0), jnp.where(low_half, 0.0, x_dt)], axis=0
        ).astype(bf16)
        y_ref[:, columns] = (
            jnp.dot(jnp.concatenate(mixing, axis=1), stacked, preferred_element_type=f32)
            + skip_ref[0:1, columns] * xc_ref[:, columns].astype(f32)
        )


def finish_kernel(
    place_ref, y_ref, bcc_ref, acum_ref, prior_ref, thr_ref, entering_ref, z_ref, gain_ref,
    weight_ref, expand_ref, out_ref, square_ref, scaled,
):
    parts = y_ref.shape[0] // CHUNK
    for part in range(parts):
        rows = slice(part * CHUNK, (part + 1) * CHUNK)
        first = place_ref[2 * PROMPTS] + (pl.program_id(0) * parts + part) * CHUNK
        token = first + rows_iota(CHUNK)
        inflow = jnp.exp(
            jnp.where(start_of(token, place_ref) < first, acum_ref[rows], NEVER)
        )
        state = (
            prior_ref[part].astype(f32)
            + spread_row(thr_ref[part, 0:1], expand_ref) * entering_ref[...]
        ).astype(bf16)
        ssm = y_ref[rows] + spread_heads(inflow, expand_ref) * jnp.dot(
            bcc_ref[rows, NS:], state, preferred_element_type=f32
        )
        z = z_ref[rows].astype(f32)
        gated = ssm * (z * jax.nn.sigmoid(z))
        square_ref[rows] = jnp.sum(gated * gated, axis=1, keepdims=True)
        scaled[rows] = (gated * gain_ref[0:1]).astype(bf16)
    block = out_ref.shape[2]
    for dest in range(out_ref.shape[0]):
        out_ref[dest] = jnp.dot(
            scaled[...],
            weight_ref[:, dest * block : (dest + 1) * block],
            preferred_element_type=f32,
        ).astype(bf16)


def whole(shape):
    return pl.BlockSpec(shape, lambda i: (0,) * len(shape))


def stepped(shape):
    return pl.BlockSpec(shape, lambda i: (i,) + (0,) * (len(shape) - 1))


smem = pl.BlockSpec(memory_space=pltpu.SMEM)


def per_device(
    hidden,
    x_weight,
    z_weight,
    bc_weight,
    dt_weight,
    conv_x,
    conv_bc,
    dt_bias,
    decay_rate,
    skip_gain,
    norm_gain,
    out_weight,
    lengths,
    owners,
):
    rows_here = hidden.shape[0]
    width = x_weight.shape[1]
    heads = dt_bias.shape[0]
    head_width = width // heads
    tp = lax.axis_size("tp")
    seq = lax.axis_size("seq")
    model = out_weight.shape[1]
    my_index = lax.axis_index("seq")
    first_row = my_index * rows_here
    prompt_end = jnp.cumsum(lengths).astype(jnp.int32)
    prompt_start = prompt_end - lengths
    place = jnp.concatenate(
        [prompt_end, prompt_start, jnp.full((8,), first_row, jnp.int32)]
    ).astype(jnp.int32)
    pad = ((0, 0), (0, LANES - heads))
    bias = jnp.broadcast_to(jnp.pad(dt_bias[None], pad), (8, LANES))
    rate = jnp.broadcast_to(jnp.pad(decay_rate[None], pad), (8, LANES))
    skip = jnp.repeat(skip_gain, head_width)[None]
    head_of = jnp.arange(width, dtype=jnp.int32) // head_width
    expand = (
        jnp.arange(2 * LANES, dtype=jnp.int32)[:, None] % LANES == head_of[None, :]
    ).astype(bf16)
    dt_wide = jnp.pad(dt_weight, pad)

    bc_full = lax.all_gather(bc_weight, "tp", axis=1, tiled=True)
    piece = lax.all_gather(hidden, "tp", axis=1, tiled=True)

    def take(rows, matrix):
        return jnp.dot(rows, matrix, preferred_element_type=f32)

    x_in = take(piece, x_weight).astype(bf16)
    bc_in = take(piece, bc_full).astype(bf16)
    tail = jnp.concatenate([x_in[rows_here - HALO :], bc_in[rows_here - HALO :]], axis=1)
    halo = lax.ppermute(tail, "seq", [(i, i + 1) for i in range(seq - 1)])
    later, unused = lax.optimization_barrier((piece, tail))
    z_in = take(later, z_weight).astype(bf16)
    dt_raw = take(later, dt_wide)

    chunks = rows_here // CHUNK
    params = pltpu.CompilerParams(
        dimension_semantics=("arbitrary",), vmem_limit_bytes=40 * 1024 * 1024
    )
    x_conv, x_dt, bc_conv, acum, prior, thr, end, finals = pl.pallas_call(
        states_kernel,
        grid=(chunks,),
        in_specs=[
            smem,
            stepped((CHUNK, width)),
            stepped((CHUNK, 2 * NS)),
            whole((HALO, width)),
            whole((HALO, 2 * NS)),
            stepped((CHUNK, LANES)),
            whole((KCONV, width)),
            whole((KCONV, 2 * NS)),
            whole((8, LANES)),
            whole((8, LANES)),
            whole((2 * LANES, width)),
        ],
        out_specs=[
            stepped((CHUNK, width)),
            stepped((CHUNK, width)),
            stepped((CHUNK, 2 * NS)),
            stepped((CHUNK, LANES)),
            stepped((1, NS, width)),
            stepped((1, 8, LANES)),
            whole((NS + EXTRA, width)),
            whole((PROMPTS, NS + EXTRA, width)),
        ],
        out_shape=[
            jax.ShapeDtypeStruct((rows_here, width), bf16),
            jax.ShapeDtypeStruct((rows_here, width), bf16),
            jax.ShapeDtypeStruct((rows_here, 2 * NS), bf16),
            jax.ShapeDtypeStruct((rows_here, LANES), f32),
            jax.ShapeDtypeStruct((chunks, NS, width), bf16),
            jax.ShapeDtypeStruct((chunks, 8, LANES), f32),
            jax.ShapeDtypeStruct((NS + EXTRA, width), bf16),
            jax.ShapeDtypeStruct((PROMPTS, NS + EXTRA, width), bf16),
        ],
        scratch_shapes=[
            pltpu.VMEM((HALO + CHUNK, width), f32),
            pltpu.VMEM((HALO + CHUNK, 2 * NS), f32),
            pltpu.VMEM((NS, width), f32),
            pltpu.VMEM((8, LANES), f32),
        ],
        compiler_params=params,
        cost_estimate=pl.CostEstimate(
            flops=8 * 10**9, bytes_accessed=16 * 10**6, transcendentals=2 * 10**6
        ),
    )(
        place, x_in, bc_in, halo[:, :width], halo[:, width:], dt_raw, conv_x, conv_bc,
        bias, rate, expand,
    )
    pieces = lax.all_gather(end, "seq")

    y = pl.pallas_call(
        within_kernel,
        grid=(chunks,),
        in_specs=[
            smem,
            stepped((CHUNK, width)),
            stepped((CHUNK, width)),
            stepped((CHUNK, 2 * NS)),
            stepped((CHUNK, LANES)),
            whole((1, width)),
        ],
        out_specs=stepped((CHUNK, width)),
        out_shape=jax.ShapeDtypeStruct((rows_here, width), f32),
        compiler_params=params,
        cost_estimate=pl.CostEstimate(
            flops=8 * 10**9, bytes_accessed=16 * 10**6, transcendentals=2 * 10**6
        ),
    )(place, x_conv, x_dt, bc_conv, acum, skip)

    def heads_of(rows, at):
        return (rows[at].astype(f32) + rows[at + 1].astype(f32))[None]

    keeper = owners[0]
    holder = (prompt_end[keeper] - 1) // rows_here
    entering = jnp.zeros((NS, width), f32)
    entering_kept = entering
    for position in range(seq - 1):
        through = heads_of(pieces[position], NS)
        local_end = pieces[position, :NS].astype(f32)
        entering = jnp.where(position < my_index, through * entering + local_end, entering)
        entering_kept = jnp.where(
            position < holder, through * entering_kept + local_end, entering_kept
        )

    wide = 2 * CHUNK
    partial, square = pl.pallas_call(
        finish_kernel,
        grid=(rows_here // wide,),
        in_specs=[
            smem,
            stepped((wide, width)),
            stepped((wide, 2 * NS)),
            stepped((wide, LANES)),
            stepped((wide // CHUNK, NS, width)),
            stepped((wide // CHUNK, 8, LANES)),
            whole((NS, width)),
            stepped((wide, width)),
            whole((1, width)),
            whole((width, model)),
            whole((2 * LANES, width)),
        ],
        out_specs=[
            pl.BlockSpec((tp, wide, model // tp), lambda i: (0, i, 0)),
            stepped((wide, 1)),
        ],
        out_shape=[
            jax.ShapeDtypeStruct((tp, rows_here, model // tp), bf16),
            jax.ShapeDtypeStruct((rows_here, 1), f32),
        ],
        scratch_shapes=[pltpu.VMEM((wide, width), bf16)],
        compiler_params=params,
        cost_estimate=pl.CostEstimate(
            flops=8 * 10**9, bytes_accessed=16 * 10**6, transcendentals=2 * 10**6
        ),
    )(
        place, y, bc_conv, acum, prior, thr, entering, z_in, norm_gain[None], out_weight, expand
    )
    summed = lax.psum_scatter(partial, "tp", scatter_dimension=0, tiled=False)
    square_sum = lax.psum(square.reshape(rows_here // LANES, LANES), "tp").reshape(rows_here, 1)
    mixed = (summed.astype(f32) * lax.rsqrt(square_sum / DIN + epsilon)).astype(bf16)

    kept = lax.psum(finals, "seq")[keeper]
    count = KCONV - 1
    final = kept[:NS].astype(f32) + heads_of(kept, NS + 2 * count) * entering_kept
    final_state = final.T.reshape(1, heads, head_width, NS)
    conv_edge_x = kept[NS : NS + count][None]
    conv_edge_bc = kept[NS + count : NS + 2 * count, : 2 * NS][None]
    return (mixed, final_state, conv_edge_x, conv_edge_bc)


def solution(mesh):
    return jax.shard_map(
        per_device,
        mesh=mesh,
        in_specs=(
            P("seq", "tp"),
            P(None, "tp"),
            P(None, "tp"),
            P(None, "tp"),
            P(None, "tp"),
            P(None, "tp"),
            P(),
            P("tp"),
            P("tp"),
            P("tp"),
            P("tp"),
            P("tp", None),
            P(),
            P("seq"),
        ),
        out_specs=(
            P("seq", "tp"),
            P("seq", "tp", None, None),
            P("seq", None, "tp"),
            P("seq", None, None),
        ),
        check_vma=False,
    )
```

```python
import functools

import jax
import jax.numpy as jnp
from jax import lax
from jax.experimental import pallas as pl
from jax.experimental.pallas import tpu as pltpu
from jax.sharding import PartitionSpec as P

NS = 128
KCONV = 4
PROMPTS = 4
DIN = 4096
CHUNK = 128
LANES = 128
HALO = 16
EXTRA = 16
NEVER = -1e30

epsilon = 1e-05
f32 = jnp.float32
bf16 = jnp.bfloat16


def rows_iota(rows, columns=LANES):
    return lax.broadcasted_iota(jnp.int32, (rows, columns), 0)


def start_of(position, place_ref):
    start = jnp.zeros_like(position)
    for r in range(PROMPTS):
        start = jnp.where(position >= place_ref[r], place_ref[r], start)
    return start


def split(value):
    high = value.astype(bf16)
    return high, (value - high.astype(f32)).astype(bf16)


def spread_heads(value, expand_ref):
    high, low = split(value)
    return jnp.dot(
        jnp.concatenate([high, low], axis=1), expand_ref[...], preferred_element_type=f32
    )


def spread_row(row, expand_ref):
    return spread_heads(jnp.broadcast_to(row, (16, LANES)), expand_ref)[0:1]


def split_rows(row, first, expand_ref):
    high, low = split(jnp.broadcast_to(row, (EXTRA, LANES)))
    at = rows_iota(EXTRA)
    both = jnp.where(at == first, high.astype(f32), 0.0) + jnp.where(
        at == first + 1, low.astype(f32), 0.0
    )
    return jnp.dot(both.astype(bf16), expand_ref[0:LANES], preferred_element_type=f32)


def conv_columns(ext_ref, taps_ref, columns, age):
    total = ext_ref[HALO : HALO + CHUNK, columns] * taps_ref[KCONV - 1 : KCONV, columns]
    for back in range(1, KCONV):
        term = (
            ext_ref[HALO - back : HALO - back + CHUNK, columns]
            * taps_ref[KCONV - 1 - back : KCONV - back, columns]
        )
        total = total + jnp.where(age >= back, term, 0.0)
    return (total * jax.nn.sigmoid(total)).astype(bf16)


def states_kernel(
    place_ref, x_ref, bc_ref, halo_x_ref, halo_bc_ref, dt_ref, taps_x_ref, taps_bc_ref,
    bias_ref, rate_ref, expand_ref,
    xc_ref, xdt_ref, bcc_ref, acum_ref, prior_ref, thr_ref, end_ref, finals_ref,
    ext_x, ext_bc, state, through,
):
    step = pl.program_id(0)
    width = x_ref.shape[1]

    @pl.when(step == 0)
    def _():
        ext_x[0:HALO] = halo_x_ref[...].astype(f32)
        ext_bc[0:HALO] = halo_bc_ref[...].astype(f32)
        state[...] = jnp.zeros_like(state)
        through[...] = jnp.ones_like(through)
        finals_ref[...] = jnp.zeros_like(finals_ref)

    @pl.when(step > 0)
    def _():
        ext_x[0:HALO] = ext_x[CHUNK : CHUNK + HALO]
        ext_bc[0:HALO] = ext_bc[CHUNK : CHUNK + HALO]

    ext_x[HALO : HALO + CHUNK] = x_ref[...].astype(f32)
    ext_bc[HALO : HALO + CHUNK] = bc_ref[...].astype(f32)

    first = place_ref[2 * PROMPTS] + step * CHUNK
    local = rows_iota(CHUNK)
    token = first + local
    age = token - start_of(token, place_ref)
    for tile in range(width // LANES):
        columns = slice(tile * LANES, (tile + 1) * LANES)
        xc_ref[:, columns] = conv_columns(ext_x, taps_x_ref, columns, age)
    for tile in range(2 * NS // LANES):
        columns = slice(tile * LANES, (tile + 1) * LANES)
        bcc_ref[:, columns] = conv_columns(ext_bc, taps_bc_ref, columns, age)

    raw = dt_ref[...] + bias_ref[0:1]
    dt = jnp.maximum(raw, 0.0) + jnp.log1p(jnp.exp(-jnp.abs(raw)))
    log_decay = -rate_ref[0:1] * dt
    lower = (
        local >= lax.broadcasted_iota(jnp.int32, (CHUNK, CHUNK), 1)
    ).astype(f32)
    acum = jnp.dot(
        lower, log_decay, precision=lax.Precision.HIGHEST, preferred_element_type=f32
    )
    acum_ref[...] = acum
    x_dt = xc_ref[...].astype(f32) * spread_heads(dt, expand_ref)
    xdt_ref[...] = x_dt.astype(bf16)
    b_turned = jnp.transpose(bcc_ref[:, 0:NS].astype(f32)).astype(bf16)
    prior_ref[0] = state[...].astype(bf16)
    thr_ref[0] = through[...]

    for r in range(PROMPTS):
        inner = place_ref[r] - 1 - first
        begin = place_ref[PROMPTS + r]

        @pl.when((inner >= 0) & (inner < CHUNK))
        def _():
            level = jnp.sum(jnp.where(local == inner, acum, 0.0), axis=0, keepdims=True)
            chosen = (local <= inner) & (token >= begin)
            weight = jnp.exp(jnp.where(chosen, level - acum, NEVER))
            enter = jnp.exp(level) * (begin < first).astype(f32)
            rows = (x_dt * spread_heads(weight, expand_ref)).astype(bf16)
            finals_ref[r, 0:NS] = (
                spread_row(enter, expand_ref) * state[...]
                + jnp.dot(b_turned, rows, preferred_element_type=f32)
            ).astype(bf16)
            at = rows_iota(EXTRA, HALO + CHUNK)
            place = lax.broadcasted_iota(jnp.int32, (EXTRA, HALO + CHUNK), 1)
            count = KCONV - 1

            def pick(skip):
                wanted = inner - (count - 1) + at - skip
                ok = (at >= skip) & (at < skip + count) & (first + wanted >= begin)
                return jnp.where(ok & (place == HALO + wanted), 1.0, 0.0).astype(bf16)

            edge_x = jnp.dot(pick(0), ext_x[...].astype(bf16), preferred_element_type=f32)
            edge_bc = jnp.dot(pick(count), ext_bc[...].astype(bf16), preferred_element_type=f32)
            edge_bc = jnp.concatenate(
                [edge_bc, jnp.zeros((EXTRA, width - 2 * NS), f32)], axis=1
            )
            passing = split_rows(through[0:1] * enter, 2 * count, expand_ref)
            finals_ref[r, NS : NS + EXTRA] = (edge_x + edge_bc + passing).astype(bf16)

    last = acum[CHUNK - 1 : CHUNK]
    closing = start_of(first + CHUNK - 1, place_ref)
    tail = jnp.exp(jnp.where(token >= closing, last - acum, NEVER))
    carry = jnp.exp(last) * (closing < first).astype(f32)
    rows = (x_dt * spread_heads(tail, expand_ref)).astype(bf16)
    state[...] = spread_row(carry, expand_ref) * state[...] + jnp.dot(
        b_turned, rows, preferred_element_type=f32
    )
    through[...] = through[...] * carry

    @pl.when(step == pl.num_programs(0) - 1)
    def _():
        end_ref[0:NS] = state[...].astype(bf16)
        owner = place_ref[2 * PROMPTS + 1].astype(f32)
        end_ref[NS : NS + EXTRA] = (
            split_rows(through[0:1], 0, expand_ref)
            + jnp.where(rows_iota(EXTRA, width) == 2, owner, 0.0)
        ).astype(bf16)


def within_kernel(place_ref, xc_ref, xdt_ref, bcc_ref, acum_ref, skip_ref, y_ref):
    width = xc_ref.shape[1]
    first = place_ref[2 * PROMPTS] + pl.program_id(0) * CHUNK
    local = rows_iota(CHUNK)
    token = first + local
    age = token - start_of(token, place_ref)
    behind = local - lax.broadcasted_iota(jnp.int32, (CHUNK, CHUNK), 1)
    bias = jnp.where((behind >= 0) & (behind <= age), 0.0, NEVER)
    scores = lax.dot_general(
        bcc_ref[:, NS:], bcc_ref[:, :NS], (((1,), (1,)), ((), ())), preferred_element_type=f32
    )
    acum = acum_ref[...]
    acum_turned = jnp.transpose(acum)
    low_half = lax.broadcasted_iota(jnp.int32, (CHUNK, LANES), 1) < LANES // 2
    for pair in range(width // LANES):
        columns = slice(pair * LANES, (pair + 1) * LANES)
        mixing = []
        for head in (2 * pair, 2 * pair + 1):
            spread = acum[:, head : head + 1] - acum_turned[head : head + 1] + bias
            mixing.append((jnp.exp(spread) * scores).astype(bf16))
        x_dt = xdt_ref[:, columns].astype(f32)
        stacked = jnp.concatenate(
            [jnp.where(low_half, x_dt, 0.0), jnp.where(low_half, 0.0, x_dt)], axis=0
        ).astype(bf16)
        y_ref[:, columns] = (
            jnp.dot(jnp.concatenate(mixing, axis=1), stacked, preferred_element_type=f32)
            + skip_ref[0:1, columns] * xc_ref[:, columns].astype(f32)
        )


def finish_kernel(
    place_ref, y_ref, bcc_ref, acum_ref, prior_ref, thr_ref, entering_ref, z_ref, gain_ref,
    weight_ref, expand_ref, out_ref, square_ref, scaled,
):
    parts = y_ref.shape[0] // CHUNK
    for part in range(parts):
        rows = slice(part * CHUNK, (part + 1) * CHUNK)
        first = place_ref[2 * PROMPTS] + (pl.program_id(0) * parts + part) * CHUNK
        token = first + rows_iota(CHUNK)
        inflow = jnp.exp(
            jnp.where(start_of(token, place_ref) < first, acum_ref[rows], NEVER)
        )
        state = (
            prior_ref[part].astype(f32)
            + spread_row(thr_ref[part, 0:1], expand_ref) * entering_ref[...]
        ).astype(bf16)
        ssm = y_ref[rows] + spread_heads(inflow, expand_ref) * jnp.dot(
            bcc_ref[rows, NS:], state, preferred_element_type=f32
        )
        z = z_ref[rows].astype(f32)
        gated = ssm * (z * jax.nn.sigmoid(z))
        square_ref[rows] = jnp.sum(gated * gated, axis=1, keepdims=True)
        scaled[rows] = (gated * gain_ref[0:1]).astype(bf16)
    block = out_ref.shape[2]
    for dest in range(out_ref.shape[0]):
        out_ref[dest] = jnp.dot(
            scaled[...],
            weight_ref[:, dest * block : (dest + 1) * block],
            preferred_element_type=f32,
        ).astype(bf16)


def whole(shape):
    return pl.BlockSpec(shape, lambda i: (0,) * len(shape))


def stepped(shape):
    return pl.BlockSpec(shape, lambda i: (i,) + (0,) * (len(shape) - 1))


smem = pl.BlockSpec(memory_space=pltpu.SMEM)


def per_device(
    hidden,
    x_weight,
    z_weight,
    bc_weight,
    dt_weight,
    conv_x,
    conv_bc,
    dt_bias,
    decay_rate,
    skip_gain,
    norm_gain,
    out_weight,
    lengths,
    owners,
):
    rows_here = hidden.shape[0]
    width = x_weight.shape[1]
    heads = dt_bias.shape[0]
    head_width = width // heads
    tp = lax.axis_size("tp")
    seq = lax.axis_size("seq")
    model = out_weight.shape[1]
    my_index = lax.axis_index("seq")
    first_row = my_index * rows_here
    prompt_end = jnp.cumsum(lengths).astype(jnp.int32)
    prompt_start = prompt_end - lengths
    place = jnp.concatenate(
        [
            prompt_end,
            prompt_start,
            jnp.full((1,), first_row, jnp.int32),
            jnp.broadcast_to(owners, (7,)),
        ]
    ).astype(jnp.int32)
    pad = ((0, 0), (0, LANES - heads))
    bias = jnp.broadcast_to(jnp.pad(dt_bias[None], pad), (8, LANES))
    rate = jnp.broadcast_to(jnp.pad(decay_rate[None], pad), (8, LANES))
    skip = jnp.repeat(skip_gain, head_width)[None]
    head_of = jnp.arange(width, dtype=jnp.int32) // head_width
    expand = (
        jnp.arange(2 * LANES, dtype=jnp.int32)[:, None] % LANES == head_of[None, :]
    ).astype(bf16)
    dt_wide = jnp.pad(dt_weight, pad)

    bc_full = lax.all_gather(bc_weight, "tp", axis=1, tiled=True)
    piece = lax.all_gather(hidden, "tp", axis=1, tiled=True)

    def take(rows, matrix):
        return jnp.dot(rows, matrix, preferred_element_type=f32)

    x_in = take(piece, x_weight).astype(bf16)
    bc_in = take(piece, bc_full).astype(bf16)
    tail = jnp.concatenate([x_in[rows_here - HALO :], bc_in[rows_here - HALO :]], axis=1)
    halo = lax.ppermute(tail, "seq", [(i, i + 1) for i in range(seq - 1)])
    later, unused = lax.optimization_barrier((piece, tail))
    z_in = take(later, z_weight).astype(bf16)
    dt_raw = take(later, dt_wide)

    chunks = rows_here // CHUNK
    params = pltpu.CompilerParams(
        dimension_semantics=("arbitrary",), vmem_limit_bytes=40 * 1024 * 1024
    )
    x_conv, x_dt, bc_conv, acum, prior, thr, end, finals = pl.pallas_call(
        states_kernel,
        grid=(chunks,),
        in_specs=[
            smem,
            stepped((CHUNK, width)),
            stepped((CHUNK, 2 * NS)),
            whole((HALO, width)),
            whole((HALO, 2 * NS)),
            stepped((CHUNK, LANES)),
            whole((KCONV, width)),
            whole((KCONV, 2 * NS)),
            whole((8, LANES)),
            whole((8, LANES)),
            whole((2 * LANES, width)),
        ],
        out_specs=[
            stepped((CHUNK, width)),
            stepped((CHUNK, width)),
            stepped((CHUNK, 2 * NS)),
            stepped((CHUNK, LANES)),
            stepped((1, NS, width)),
            stepped((1, 8, LANES)),
            whole((NS + EXTRA, width)),
            whole((PROMPTS, NS + EXTRA, width)),
        ],
        out_shape=[
            jax.ShapeDtypeStruct((rows_here, width), bf16),
            jax.ShapeDtypeStruct((rows_here, width), bf16),
            jax.ShapeDtypeStruct((rows_here, 2 * NS), bf16),
            jax.ShapeDtypeStruct((rows_here, LANES), f32),
            jax.ShapeDtypeStruct((chunks, NS, width), bf16),
            jax.ShapeDtypeStruct((chunks, 8, LANES), f32),
            jax.ShapeDtypeStruct((NS + EXTRA, width), bf16),
            jax.ShapeDtypeStruct((PROMPTS, NS + EXTRA, width), bf16),
        ],
        scratch_shapes=[
            pltpu.VMEM((HALO + CHUNK, width), f32),
            pltpu.VMEM((HALO + CHUNK, 2 * NS), f32),
            pltpu.VMEM((NS, width), f32),
            pltpu.VMEM((8, LANES), f32),
        ],
        compiler_params=params,
        cost_estimate=pl.CostEstimate(
            flops=8 * 10**9, bytes_accessed=16 * 10**6, transcendentals=2 * 10**6
        ),
    )(
        place, x_in, bc_in, halo[:, :width], halo[:, width:], dt_raw, conv_x, conv_bc,
        bias, rate, expand,
    )
    pieces = lax.all_gather(end, "seq")

    y = pl.pallas_call(
        within_kernel,
        grid=(chunks,),
        in_specs=[
            smem,
            stepped((CHUNK, width)),
            stepped((CHUNK, width)),
            stepped((CHUNK, 2 * NS)),
            stepped((CHUNK, LANES)),
            whole((1, width)),
        ],
        out_specs=stepped((CHUNK, width)),
        out_shape=jax.ShapeDtypeStruct((rows_here, width), f32),
        compiler_params=params,
        cost_estimate=pl.CostEstimate(
            flops=8 * 10**9, bytes_accessed=16 * 10**6, transcendentals=2 * 10**6
        ),
    )(place, x_conv, x_dt, bc_conv, acum, skip)

    def heads_of(rows, at):
        return (rows[at].astype(f32) + rows[at + 1].astype(f32))[None]

    keeper = owners[0]
    holder = (prompt_end[keeper] - 1) // rows_here
    entering = jnp.zeros((NS, width), f32)
    entering_kept = entering
    for position in range(seq - 1):
        through = heads_of(pieces[position], NS)
        local_end = pieces[position, :NS].astype(f32)
        entering = jnp.where(position < my_index, through * entering + local_end, entering)
        entering_kept = jnp.where(
            position < holder, through * entering_kept + local_end, entering_kept
        )

    wide = 2 * CHUNK
    partial, square = pl.pallas_call(
        finish_kernel,
        grid=(rows_here // wide,),
        in_specs=[
            smem,
            stepped((wide, width)),
            stepped((wide, 2 * NS)),
            stepped((wide, LANES)),
            stepped((wide // CHUNK, NS, width)),
            stepped((wide // CHUNK, 8, LANES)),
            whole((NS, width)),
            stepped((wide, width)),
            whole((1, width)),
            whole((width, model)),
            whole((2 * LANES, width)),
        ],
        out_specs=[
            pl.BlockSpec((tp, wide, model // tp), lambda i: (0, i, 0)),
            stepped((wide, 1)),
        ],
        out_shape=[
            jax.ShapeDtypeStruct((tp, rows_here, model // tp), bf16),
            jax.ShapeDtypeStruct((rows_here, 1), f32),
        ],
        scratch_shapes=[pltpu.VMEM((wide, width), bf16)],
        compiler_params=params,
        cost_estimate=pl.CostEstimate(
            flops=8 * 10**9, bytes_accessed=16 * 10**6, transcendentals=2 * 10**6
        ),
    )(
        place, y, bc_conv, acum, prior, thr, entering, z_in, norm_gain[None], out_weight, expand
    )
    summed = lax.psum_scatter(partial, "tp", scatter_dimension=0, tiled=False)
    square_sum = lax.psum(square.reshape(rows_here // LANES, LANES), "tp").reshape(rows_here, 1)
    mixed = (summed.astype(f32) * lax.rsqrt(square_sum / DIN + epsilon)).astype(bf16)

    wanted = pieces[:, NS + 2, 0].astype(jnp.int32)

    def slots_for(prompts):
        chosen = prompts[:, None, None]
        total = jnp.where(chosen == 0, finals[0][None], jnp.zeros((), bf16))
        for r in range(1, PROMPTS):
            total = jnp.where(chosen == r, finals[r][None], total)
        return total

    slots = None
    for bit in range(seq.bit_length() - 1):
        mine = (my_index >> bit) & 1
        if bit == 0:
            pairs = wanted.reshape(seq // 2, 2)
            own = slots_for(jnp.where(mine == 0, pairs[:, 0], pairs[:, 1]))
            sent = slots_for(jnp.where(mine == 0, pairs[:, 1], pairs[:, 0]))
        else:
            pairs = slots.reshape((slots.shape[0] // 2, 2) + slots.shape[1:])
            own = jnp.where(mine == 0, pairs[:, 0], pairs[:, 1])
            sent = jnp.where(mine == 0, pairs[:, 1], pairs[:, 0])
        partners = [(i, i ^ (1 << bit)) for i in range(seq)]
        slots = own + lax.ppermute(sent, "seq", partners)
    kept = slots[0]
    count = KCONV - 1
    final = kept[:NS].astype(f32) + heads_of(kept, NS + 2 * count) * entering_kept
    final_state = final.T.reshape(1, heads, head_width, NS)
    conv_edge_x = kept[NS : NS + count][None]
    conv_edge_bc = kept[NS + count : NS + 2 * count, : 2 * NS][None]
    return (mixed, final_state, conv_edge_x, conv_edge_bc)


def solution(mesh):
    return jax.shard_map(
        per_device,
        mesh=mesh,
        in_specs=(
            P("seq", "tp"),
            P(None, "tp"),
            P(None, "tp"),
            P(None, "tp"),
            P(None, "tp"),
            P(None, "tp"),
            P(),
            P("tp"),
            P("tp"),
            P("tp"),
            P("tp"),
            P("tp", None),
            P(),
            P("seq"),
        ),
        out_specs=(
            P("seq", "tp"),
            P("seq", "tp", None, None),
            P("seq", None, "tp"),
            P("seq", None, None),
        ),
        check_vma=False,
    )
```

```python
import functools

import jax
import jax.numpy as jnp
from jax import lax
from jax.experimental import pallas as pl
from jax.experimental.pallas import tpu as pltpu
from jax.sharding import PartitionSpec as P

NS = 128
KCONV = 4
PROMPTS = 4
DIN = 4096
CHUNK = 128
LANES = 128
HALO = 16
EXTRA = 16
NEVER = -1e30

epsilon = 1e-05
f32 = jnp.float32
bf16 = jnp.bfloat16


def rows_iota(rows, columns=LANES):
    return lax.broadcasted_iota(jnp.int32, (rows, columns), 0)


def start_of(position, place_ref):
    start = jnp.zeros_like(position)
    for r in range(PROMPTS):
        start = jnp.where(position >= place_ref[r], place_ref[r], start)
    return start


def split(value):
    high = value.astype(bf16)
    return high, (value - high.astype(f32)).astype(bf16)


def spread_heads(value, expand_ref):
    high, low = split(value)
    return jnp.dot(
        jnp.concatenate([high, low], axis=1), expand_ref[...], preferred_element_type=f32
    )


def spread_row(row, expand_ref):
    return spread_heads(jnp.broadcast_to(row, (16, LANES)), expand_ref)[0:1]


def split_rows(row, first, expand_ref):
    high, low = split(jnp.broadcast_to(row, (EXTRA, LANES)))
    at = rows_iota(EXTRA)
    both = jnp.where(at == first, high.astype(f32), 0.0) + jnp.where(
        at == first + 1, low.astype(f32), 0.0
    )
    return jnp.dot(both.astype(bf16), expand_ref[0:LANES], preferred_element_type=f32)


def conv_columns(ext_ref, taps_ref, columns, age):
    total = ext_ref[HALO : HALO + CHUNK, columns] * taps_ref[KCONV - 1 : KCONV, columns]
    for back in range(1, KCONV):
        term = (
            ext_ref[HALO - back : HALO - back + CHUNK, columns]
            * taps_ref[KCONV - 1 - back : KCONV - back, columns]
        )
        total = total + jnp.where(age >= back, term, 0.0)
    return (total * jax.nn.sigmoid(total)).astype(bf16)


def states_kernel(
    place_ref, x_ref, bc_ref, halo_x_ref, halo_bc_ref, dt_ref, taps_x_ref, taps_bc_ref,
    bias_ref, rate_ref, expand_ref,
    xc_ref, xdt_ref, bcc_ref, acum_ref, prior_ref, thr_ref, end_ref, finals_ref,
    ext_x, ext_bc, state, through,
):
    step = pl.program_id(0)
    width = x_ref.shape[1]

    @pl.when(step == 0)
    def _():
        ext_x[0:HALO] = halo_x_ref[...].astype(f32)
        ext_bc[0:HALO] = halo_bc_ref[...].astype(f32)
        state[...] = jnp.zeros_like(state)
        through[...] = jnp.ones_like(through)
        finals_ref[...] = jnp.zeros_like(finals_ref)

    @pl.when(step > 0)
    def _():
        ext_x[0:HALO] = ext_x[CHUNK : CHUNK + HALO]
        ext_bc[0:HALO] = ext_bc[CHUNK : CHUNK + HALO]

    ext_x[HALO : HALO + CHUNK] = x_ref[...].astype(f32)
    ext_bc[HALO : HALO + CHUNK] = bc_ref[...].astype(f32)

    first = place_ref[2 * PROMPTS] + step * CHUNK
    local = rows_iota(CHUNK)
    token = first + local
    age = token - start_of(token, place_ref)
    for tile in range(width // LANES):
        columns = slice(tile * LANES, (tile + 1) * LANES)
        xc_ref[:, columns] = conv_columns(ext_x, taps_x_ref, columns, age)
    for tile in range(2 * NS // LANES):
        columns = slice(tile * LANES, (tile + 1) * LANES)
        bcc_ref[:, columns] = conv_columns(ext_bc, taps_bc_ref, columns, age)

    raw = dt_ref[...] + bias_ref[0:1]
    dt = jnp.maximum(raw, 0.0) + jnp.log1p(jnp.exp(-jnp.abs(raw)))
    log_decay = -rate_ref[0:1] * dt
    lower = (
        local >= lax.broadcasted_iota(jnp.int32, (CHUNK, CHUNK), 1)
    ).astype(f32)
    acum = jnp.dot(
        lower, log_decay, precision=lax.Precision.HIGHEST, preferred_element_type=f32
    )
    acum_ref[...] = acum
    x_dt = xc_ref[...].astype(f32) * spread_heads(dt, expand_ref)
    xdt_ref[...] = x_dt.astype(bf16)
    b_turned = jnp.transpose(bcc_ref[:, 0:NS].astype(f32)).astype(bf16)
    prior_ref[0] = state[...].astype(bf16)
    thr_ref[0] = through[...]

    for r in range(PROMPTS):
        inner = place_ref[r] - 1 - first
        begin = place_ref[PROMPTS + r]

        @pl.when((inner >= 0) & (inner < CHUNK))
        def _():
            level = jnp.sum(jnp.where(local == inner, acum, 0.0), axis=0, keepdims=True)
            chosen = (local <= inner) & (token >= begin)
            weight = jnp.exp(jnp.where(chosen, level - acum, NEVER))
            enter = jnp.exp(level) * (begin < first).astype(f32)
            rows = (x_dt * spread_heads(weight, expand_ref)).astype(bf16)
            finals_ref[r, 0:NS] = (
                spread_row(enter, expand_ref) * state[...]
                + jnp.dot(b_turned, rows, preferred_element_type=f32)
            ).astype(bf16)
            at = rows_iota(EXTRA, HALO + CHUNK)
            place = lax.broadcasted_iota(jnp.int32, (EXTRA, HALO + CHUNK), 1)
            count = KCONV - 1

            def pick(skip):
                wanted = inner - (count - 1) + at - skip
                ok = (at >= skip) & (at < skip + count) & (first + wanted >= begin)
                return jnp.where(ok & (place == HALO + wanted), 1.0, 0.0).astype(bf16)

            edge_x = jnp.dot(pick(0), ext_x[...].astype(bf16), preferred_element_type=f32)
            edge_bc = jnp.dot(pick(count), ext_bc[...].astype(bf16), preferred_element_type=f32)
            edge_bc = jnp.concatenate(
                [edge_bc, jnp.zeros((EXTRA, width - 2 * NS), f32)], axis=1
            )
            passing = split_rows(through[0:1] * enter, 2 * count, expand_ref)
            finals_ref[r, NS : NS + EXTRA] = (edge_x + edge_bc + passing).astype(bf16)

    last = acum[CHUNK - 1 : CHUNK]
    closing = start_of(first + CHUNK - 1, place_ref)
    tail = jnp.exp(jnp.where(token >= closing, last - acum, NEVER))
    carry = jnp.exp(last) * (closing < first).astype(f32)
    rows = (x_dt * spread_heads(tail, expand_ref)).astype(bf16)
    state[...] = spread_row(carry, expand_ref) * state[...] + jnp.dot(
        b_turned, rows, preferred_element_type=f32
    )
    through[...] = through[...] * carry

    @pl.when(step == pl.num_programs(0) - 1)
    def _():
        end_ref[0:NS] = state[...].astype(bf16)
        owner = place_ref[2 * PROMPTS + 1].astype(f32)
        end_ref[NS : NS + EXTRA] = (
            split_rows(through[0:1], 0, expand_ref)
            + jnp.where(rows_iota(EXTRA, width) == 2, owner, 0.0)
        ).astype(bf16)


def within_kernel(place_ref, xc_ref, xdt_ref, bcc_ref, acum_ref, skip_ref, y_ref):
    width = xc_ref.shape[1]
    first = place_ref[2 * PROMPTS] + pl.program_id(0) * CHUNK
    local = rows_iota(CHUNK)
    token = first + local
    age = token - start_of(token, place_ref)
    behind = local - lax.broadcasted_iota(jnp.int32, (CHUNK, CHUNK), 1)
    bias = jnp.where((behind >= 0) & (behind <= age), 0.0, NEVER)
    scores = lax.dot_general(
        bcc_ref[:, NS:], bcc_ref[:, :NS], (((1,), (1,)), ((), ())), preferred_element_type=f32
    )
    acum = acum_ref[...]
    acum_turned = jnp.transpose(acum)
    low_half = lax.broadcasted_iota(jnp.int32, (CHUNK, LANES), 1) < LANES // 2
    for pair in range(width // LANES):
        columns = slice(pair * LANES, (pair + 1) * LANES)
        mixing = []
        for head in (2 * pair, 2 * pair + 1):
            spread = acum[:, head : head + 1] - acum_turned[head : head + 1] + bias
            mixing.append((jnp.exp(spread) * scores).astype(bf16))
        x_dt = xdt_ref[:, columns].astype(f32)
        stacked = jnp.concatenate(
            [jnp.where(low_half, x_dt, 0.0), jnp.where(low_half, 0.0, x_dt)], axis=0
        ).astype(bf16)
        y_ref[:, columns] = (
            jnp.dot(jnp.concatenate(mixing, axis=1), stacked, preferred_element_type=f32)
            + skip_ref[0:1, columns] * xc_ref[:, columns].astype(f32)
        )


def finish_kernel(
    place_ref, y_ref, bcc_ref, acum_ref, prior_ref, thr_ref, entering_ref, z_ref, gain_ref,
    weight_ref, expand_ref, out_ref, square_ref, scaled,
):
    parts = y_ref.shape[0] // CHUNK
    for part in range(parts):
        rows = slice(part * CHUNK, (part + 1) * CHUNK)
        first = place_ref[2 * PROMPTS] + (pl.program_id(0) * parts + part) * CHUNK
        token = first + rows_iota(CHUNK)
        inflow = jnp.exp(
            jnp.where(start_of(token, place_ref) < first, acum_ref[rows], NEVER)
        )
        state = (
            prior_ref[part].astype(f32)
            + spread_row(thr_ref[part, 0:1], expand_ref) * entering_ref[...]
        ).astype(bf16)
        ssm = y_ref[rows] + spread_heads(inflow, expand_ref) * jnp.dot(
            bcc_ref[rows, NS:], state, preferred_element_type=f32
        )
        z = z_ref[rows].astype(f32)
        gated = ssm * (z * jax.nn.sigmoid(z))
        square_ref[rows] = jnp.sum(gated * gated, axis=1, keepdims=True)
        scaled[rows] = (gated * gain_ref[0:1]).astype(bf16)
    block = out_ref.shape[2]
    for dest in range(out_ref.shape[0]):
        out_ref[dest] = jnp.dot(
            scaled[...],
            weight_ref[:, dest * block : (dest + 1) * block],
            preferred_element_type=f32,
        ).astype(bf16)


def whole(shape):
    return pl.BlockSpec(shape, lambda i: (0,) * len(shape))


def stepped(shape):
    return pl.BlockSpec(shape, lambda i: (i,) + (0,) * (len(shape) - 1))


smem = pl.BlockSpec(memory_space=pltpu.SMEM)


def per_device(
    hidden,
    x_weight,
    z_weight,
    bc_weight,
    dt_weight,
    conv_x,
    conv_bc,
    dt_bias,
    decay_rate,
    skip_gain,
    norm_gain,
    out_weight,
    lengths,
    owners,
):
    rows_here = hidden.shape[0]
    width = x_weight.shape[1]
    heads = dt_bias.shape[0]
    head_width = width // heads
    tp = lax.axis_size("tp")
    seq = lax.axis_size("seq")
    model = out_weight.shape[1]
    my_index = lax.axis_index("seq")
    first_row = my_index * rows_here
    prompt_end = jnp.cumsum(lengths).astype(jnp.int32)
    prompt_start = prompt_end - lengths
    place = jnp.concatenate(
        [
            prompt_end,
            prompt_start,
            jnp.full((1,), first_row, jnp.int32),
            jnp.broadcast_to(owners, (7,)),
        ]
    ).astype(jnp.int32)
    pad = ((0, 0), (0, LANES - heads))
    bias = jnp.broadcast_to(jnp.pad(dt_bias[None], pad), (8, LANES))
    rate = jnp.broadcast_to(jnp.pad(decay_rate[None], pad), (8, LANES))
    skip = jnp.repeat(skip_gain, head_width)[None]
    head_of = jnp.arange(width, dtype=jnp.int32) // head_width
    expand = (
        jnp.arange(2 * LANES, dtype=jnp.int32)[:, None] % LANES == head_of[None, :]
    ).astype(bf16)
    dt_wide = jnp.pad(dt_weight, pad)

    bc_full = lax.all_gather(bc_weight, "tp", axis=1, tiled=True)
    mine_tp = lax.axis_index("tp")
    blocks = [hidden]
    apart = [0]
    bit = tp // 2
    while bit:
        partners = [(i, i ^ bit) for i in range(tp)]
        blocks = blocks + [lax.ppermute(block, "tp", partners) for block in blocks]
        apart = apart + [distance ^ bit for distance in apart]
        bit //= 2
    share = hidden.shape[1]
    piece = jnp.zeros((rows_here, tp * share), bf16)
    for block, distance in zip(blocks, apart):
        piece = lax.dynamic_update_slice_in_dim(piece, block, (mine_tp ^ distance) * share, 1)

    def take(rows, matrix):
        return jnp.dot(rows, matrix, preferred_element_type=f32)

    x_in = take(piece, x_weight).astype(bf16)
    bc_in = take(piece, bc_full).astype(bf16)
    tail = jnp.concatenate([x_in[rows_here - HALO :], bc_in[rows_here - HALO :]], axis=1)
    halo = lax.ppermute(tail, "seq", [(i, i + 1) for i in range(seq - 1)])
    later, unused = lax.optimization_barrier((piece, tail))
    z_in = take(later, z_weight).astype(bf16)
    dt_raw = take(later, dt_wide)

    chunks = rows_here // CHUNK
    params = pltpu.CompilerParams(
        dimension_semantics=("arbitrary",), vmem_limit_bytes=40 * 1024 * 1024
    )
    x_conv, x_dt, bc_conv, acum, prior, thr, end, finals = pl.pallas_call(
        states_kernel,
        grid=(chunks,),
        in_specs=[
            smem,
            stepped((CHUNK, width)),
            stepped((CHUNK, 2 * NS)),
            whole((HALO, width)),
            whole((HALO, 2 * NS)),
            stepped((CHUNK, LANES)),
            whole((KCONV, width)),
            whole((KCONV, 2 * NS)),
            whole((8, LANES)),
            whole((8, LANES)),
            whole((2 * LANES, width)),
        ],
        out_specs=[
            stepped((CHUNK, width)),
            stepped((CHUNK, width)),
            stepped((CHUNK, 2 * NS)),
            stepped((CHUNK, LANES)),
            stepped((1, NS, width)),
            stepped((1, 8, LANES)),
            whole((NS + EXTRA, width)),
            whole((PROMPTS, NS + EXTRA, width)),
        ],
        out_shape=[
            jax.ShapeDtypeStruct((rows_here, width), bf16),
            jax.ShapeDtypeStruct((rows_here, width), bf16),
            jax.ShapeDtypeStruct((rows_here, 2 * NS), bf16),
            jax.ShapeDtypeStruct((rows_here, LANES), f32),
            jax.ShapeDtypeStruct((chunks, NS, width), bf16),
            jax.ShapeDtypeStruct((chunks, 8, LANES), f32),
            jax.ShapeDtypeStruct((NS + EXTRA, width), bf16),
            jax.ShapeDtypeStruct((PROMPTS, NS + EXTRA, width), bf16),
        ],
        scratch_shapes=[
            pltpu.VMEM((HALO + CHUNK, width), f32),
            pltpu.VMEM((HALO + CHUNK, 2 * NS), f32),
            pltpu.VMEM((NS, width), f32),
            pltpu.VMEM((8, LANES), f32),
        ],
        compiler_params=params,
        cost_estimate=pl.CostEstimate(
            flops=8 * 10**9, bytes_accessed=16 * 10**6, transcendentals=2 * 10**6
        ),
    )(
        place, x_in, bc_in, halo[:, :width], halo[:, width:], dt_raw, conv_x, conv_bc,
        bias, rate, expand,
    )
    pieces = lax.all_gather(end, "seq")

    y = pl.pallas_call(
        within_kernel,
        grid=(chunks,),
        in_specs=[
            smem,
            stepped((CHUNK, width)),
            stepped((CHUNK, width)),
            stepped((CHUNK, 2 * NS)),
            stepped((CHUNK, LANES)),
            whole((1, width)),
        ],
        out_specs=stepped((CHUNK, width)),
        out_shape=jax.ShapeDtypeStruct((rows_here, width), f32),
        compiler_params=params,
        cost_estimate=pl.CostEstimate(
            flops=8 * 10**9, bytes_accessed=16 * 10**6, transcendentals=2 * 10**6
        ),
    )(place, x_conv, x_dt, bc_conv, acum, skip)

    def heads_of(rows, at):
        return (rows[at].astype(f32) + rows[at + 1].astype(f32))[None]

    keeper = owners[0]
    holder = (prompt_end[keeper] - 1) // rows_here
    entering = jnp.zeros((NS, width), f32)
    entering_kept = entering
    for position in range(seq - 1):
        through = heads_of(pieces[position], NS)
        local_end = pieces[position, :NS].astype(f32)
        entering = jnp.where(position < my_index, through * entering + local_end, entering)
        entering_kept = jnp.where(
            position < holder, through * entering_kept + local_end, entering_kept
        )

    wide = 2 * CHUNK
    partial, square = pl.pallas_call(
        finish_kernel,
        grid=(rows_here // wide,),
        in_specs=[
            smem,
            stepped((wide, width)),
            stepped((wide, 2 * NS)),
            stepped((wide, LANES)),
            stepped((wide // CHUNK, NS, width)),
            stepped((wide // CHUNK, 8, LANES)),
            whole((NS, width)),
            stepped((wide, width)),
            whole((1, width)),
            whole((width, model)),
            whole((2 * LANES, width)),
        ],
        out_specs=[
            pl.BlockSpec((tp, wide, model // tp), lambda i: (0, i, 0)),
            stepped((wide, 1)),
        ],
        out_shape=[
            jax.ShapeDtypeStruct((tp, rows_here, model // tp), bf16),
            jax.ShapeDtypeStruct((rows_here, 1), f32),
        ],
        scratch_shapes=[pltpu.VMEM((wide, width), bf16)],
        compiler_params=params,
        cost_estimate=pl.CostEstimate(
            flops=8 * 10**9, bytes_accessed=16 * 10**6, transcendentals=2 * 10**6
        ),
    )(
        place, y, bc_conv, acum, prior, thr, entering, z_in, norm_gain[None], out_weight, expand
    )
    summed = lax.psum_scatter(partial, "tp", scatter_dimension=0, tiled=False)
    square_sum = lax.psum(square.reshape(rows_here // LANES, LANES), "tp").reshape(rows_here, 1)
    mixed = (summed.astype(f32) * lax.rsqrt(square_sum / DIN + epsilon)).astype(bf16)

    wanted = pieces[:, NS + 2, 0].astype(jnp.int32)

    def slots_for(prompts):
        chosen = prompts[:, None, None]
        total = jnp.where(chosen == 0, finals[0][None], jnp.zeros((), bf16))
        for r in range(1, PROMPTS):
            total = jnp.where(chosen == r, finals[r][None], total)
        return total

    slots = None
    for bit in range(seq.bit_length() - 1):
        mine = (my_index >> bit) & 1
        if bit == 0:
            pairs = wanted.reshape(seq // 2, 2)
            own = slots_for(jnp.where(mine == 0, pairs[:, 0], pairs[:, 1]))
            sent = slots_for(jnp.where(mine == 0, pairs[:, 1], pairs[:, 0]))
        else:
            pairs = slots.reshape((slots.shape[0] // 2, 2) + slots.shape[1:])
            own = jnp.where(mine == 0, pairs[:, 0], pairs[:, 1])
            sent = jnp.where(mine == 0, pairs[:, 1], pairs[:, 0])
        partners = [(i, i ^ (1 << bit)) for i in range(seq)]
        slots = own + lax.ppermute(sent, "seq", partners)
    kept = slots[0]
    count = KCONV - 1
    final = kept[:NS].astype(f32) + heads_of(kept, NS + 2 * count) * entering_kept
    final_state = final.T.reshape(1, heads, head_width, NS)
    conv_edge_x = kept[NS : NS + count][None]
    conv_edge_bc = kept[NS + count : NS + 2 * count, : 2 * NS][None]
    return (mixed, final_state, conv_edge_x, conv_edge_bc)


def solution(mesh):
    return jax.shard_map(
        per_device,
        mesh=mesh,
        in_specs=(
            P("seq", "tp"),
            P(None, "tp"),
            P(None, "tp"),
            P(None, "tp"),
            P(None, "tp"),
            P(None, "tp"),
            P(),
            P("tp"),
            P("tp"),
            P("tp"),
            P("tp"),
            P("tp", None),
            P(),
            P("seq"),
        ),
        out_specs=(
            P("seq", "tp"),
            P("seq", "tp", None, None),
            P("seq", None, "tp"),
            P("seq", None, None),
        ),
        check_vma=False,
    )
```
